1024 devices in a mesh: section: 16 (over z_lo, x), tensor: 16 (over y, core), dp: 4 (over z_hi).
Axes of the slice: x: 8, y: 8, z: 8 (z_hi: 4, z_lo: 2; z = z_hi * 2 + z_lo), core: 2. Of those that a mesh axis runs over, the one named last changes fastest.
Arguments:
- weights: bfloat16 [16, 8192, 8192], P('section', 'tensor'), may hold values from -0.09375 to 0.09375
- contexts: bfloat16 [16, 4, 512, 8192], P('section', None, 'dp', 'tensor'), may hold values from -6 to 6
- residual: bfloat16 [16, 4, 512, 8192], P('section', None, 'dp', 'tensor'), may hold values from -6 to 6
- plan: int32 [16], P('section'), may hold values from 0 to 3, as said below
- upstream: bfloat16 [16, 512, 8192], P('section', 'dp', 'tensor'), may hold values from -6 to 6
Outputs:
- boundary: bfloat16 [16, 512, 8192], P('section', 'dp', 'tensor')
- ctx_grad: bfloat16 [16, 512, 8192], P('section', 'dp', 'tensor')
The draws below stay inside these ranges and needn't reach their ends.
Inputs may be any that keep to these rules, and one draw needn't show every extreme that they name: `plan`: some section names micro-batch 0 and some other section names micro-batch 4 - 1.
All inputs are finite; a program needn't handle non-finite values.
Results may differ from the reference program's by a relative error of at most 0.001.
Values may be sent and summed in bfloat16 or wider, within the bound.
No kernel may reach another device: no remote copies, remote signals or barrier semaphores. Data moves between devices by JAX's collectives and lax.ppermute only.
A program may use at most 64 MiB of HBM per device.

```python
import jax
import jax.numpy as jnp
from jax import lax

D = 8192
MICRO = 4
TOKENS = 512
SECTIONS = 16


def draw_plan(key, part):
    key = jax.random.fold_in(key, 11)
    first_key, second_key = jax.random.split(key)
    picks = jax.random.randint(first_key, (SECTIONS,), 0, MICRO).astype(jnp.int32)
    places = jax.random.permutation(second_key, SECTIONS).astype(jnp.int32)
    picks = picks.at[places[0]].set(0)
    picks = picks.at[places[1]].set(MICRO - 1)
    return picks.astype(jnp.int32)


def spiked(array, stream_key, source, target, parts, factor):
    def block_of(axis_at):
        return (jnp.arange(array.shape[axis_at]) // (array.shape[axis_at] // parts)).reshape((-1,) + (1,) * (array.ndim - 1 - axis_at))

    first = jax.random.permutation(stream_key, parts)[block_of(target)]
    other_side = (block_of(target) + parts // 2) % parts
    return jnp.where((block_of(source) == first) | (block_of(source) == other_side), factor * array, array)


def shard_levels(stream_key, shape, pieces, smallest, top_value):
    level = 1.0
    for position, blocks in pieces:
        steps = jax.random.uniform(jax.random.fold_in(jax.random.fold_in(stream_key, 6), position), (blocks,), jnp.float32, smallest / len(pieces), top_value / len(pieces))
        level = level * jnp.repeat(jnp.exp(steps), shape[position] // blocks).reshape((-1,) + (1,) * (len(shape) - 1 - position))
    return level


def scatter_about(rng, shape, spread, bound, shards=(), dtype=jnp.bfloat16):
    values = spread * jax.random.normal(rng, shape, jnp.float32)
    if shards:
        values = values * shard_levels(rng, shape, shards, -0.22, 0.18)
    return jnp.clip(values, -bound, bound).astype(dtype)


def bell_draw_with(stream_key, dims, scale, bound, cuts, heavy, kind=jnp.bfloat16):
    result = scale * jax.random.normal(stream_key, dims, jnp.float32)
    if cuts:
        result = result * shard_levels(stream_key, dims, cuts, -0.22, 0.18)
    return jnp.clip(spiked(result, jax.random.fold_in(stream_key, 3), *heavy), -bound, bound).astype(kind)


def setup_inputs(seed: int = 0) -> dict:
    streams_of = jax.random.split(jax.random.key(seed), 6)
    return {
        "weights": bell_draw_with(streams_of[0], (SECTIONS, D, D), D ** -0.5, 0.09375, ((0, 16), (1, 16)), (1, 2, 16, 2.0)),
        "contexts": scatter_about(streams_of[1], (SECTIONS, MICRO, TOKENS, D), 1.0, 6.0, ((0, 16), (2, 4), (3, 16))),
        "residual": scatter_about(streams_of[2], (SECTIONS, MICRO, TOKENS, D), 1.0, 6.0, ((0, 16), (2, 4), (3, 16))),
        "plan": draw_plan(jax.random.fold_in(streams_of[5], 71), 0),
        "upstream": scatter_about(streams_of[4], (SECTIONS, TOKENS, D), 1.0, 6.0, ((0, 16), (1, 4), (2, 16))),
    }


def reference(weights, contexts, residual, plan, upstream):
    def forward(section_args):
        w_section, ctx_section, res_section, chosen = section_args
        context = lax.dynamic_index_in_dim(ctx_section, chosen, 0, keepdims=False)
        stream = lax.dynamic_index_in_dim(res_section, chosen, 0, keepdims=False)
        projected = jnp.dot(context, w_section, preferred_element_type=jnp.float32)
        return (stream.astype(jnp.float32) + projected).astype(jnp.bfloat16)

    hidden = lax.map(forward, (weights, contexts, residual, plan))
    boundary = jnp.roll(hidden, 1, axis=0)
    incoming = jnp.roll(upstream, -1, axis=0)

    def backward(section_args):
        grad_in, w_section = section_args
        return jnp.dot(grad_in, w_section.T, preferred_element_type=jnp.float32).astype(jnp.bfloat16)

    ctx_grad = lax.map(backward, (incoming, weights))
    return boundary, ctx_grad
```

```python
import functools

import jax
import jax.numpy as jnp
from jax import lax
from jax.experimental import pallas as pl
from jax.experimental.pallas import tpu as pltpu
from jax.sharding import PartitionSpec as P

ROWS = 128
WIDE = 1024
LEVELS = 32700.0


def split_shift(value, by):
    peers = lax.axis_size("tensor")
    chips = peers // 2
    pairs = []
    for chip in range(chips):
        pairs.append((2 * chip, 2 * ((chip + by) % chips)))
        pairs.append((2 * chip + 1, 2 * ((chip - by) % chips) + 1))
    return lax.ppermute(value, "tensor", pairs)


def core_swap(value):
    peers = lax.axis_size("tensor")
    return lax.ppermute(value, "tensor", [(i, i ^ 1) for i in range(peers)])


def next_section(value, by, flip=False):
    sections, peers = lax.axis_size("section"), lax.axis_size("tensor")
    pairs = [
        (s * peers + t, ((s + by) % sections) * peers + (t ^ 1 if flip else t))
        for s in range(sections)
        for t in range(peers)
    ]
    return lax.ppermute(value, ("section", "tensor"), pairs)


def project(order, context, weights, count):
    def body(order_ref, ctx_ref, w_ref, out_ref):
        out_ref[0] = jnp.dot(ctx_ref[...], w_ref[...], preferred_element_type=jnp.float32)

    heads = context.shape[1]
    return pl.pallas_call(
        body,
        grid_spec=pltpu.PrefetchScalarGridSpec(
            num_scalar_prefetch=1,
            grid=(count,),
            in_specs=[
                pl.BlockSpec((ROWS, heads), lambda k, o: (0, 0)),
                pl.BlockSpec((heads, WIDE), lambda k, o: (0, o[k])),
            ],
            out_specs=pl.BlockSpec((1, ROWS, WIDE), lambda k, o: (k, 0, 0)),
        ),
        out_shape=jax.ShapeDtypeStruct((count, ROWS, WIDE), jnp.float32),
        cost_estimate=pl.CostEstimate(
            flops=2 * count * ROWS * heads * WIDE,
            bytes_accessed=count * WIDE * (2 * heads + 4 * ROWS),
            transcendentals=0,
        ),
    )(order, context, weights)


def backproject(order, parts, start, weights):
    count = len(parts)
    heads = weights.shape[0]

    def body(order_ref, *refs):
        lhs, w_ref, out_ref = refs[:count], refs[-2], refs[-1]
        step = pl.program_id(0)

        @pl.when(step == 0)
        def _():
            if start is None:
                out_ref[...] = jnp.zeros_like(out_ref)
            else:
                out_ref[...] = refs[count][...]

        for k in range(count):

            @pl.when(step == k)
            def _(k=k):
                out_ref[...] += lax.dot_general(
                    lhs[k][...],
                    w_ref[...],
                    (((1,), (1,)), ((), ())),
                    preferred_element_type=jnp.float32,
                )

    whole = pl.BlockSpec((ROWS, WIDE), lambda k, o: (0, 0))
    total = pl.BlockSpec((ROWS, heads), lambda k, o: (0, 0))
    extra = [] if start is None else [start]
    return pl.pallas_call(
        body,
        grid_spec=pltpu.PrefetchScalarGridSpec(
            num_scalar_prefetch=1,
            grid=(count,),
            in_specs=[whole] * count
            + [total] * len(extra)
            + [pl.BlockSpec((heads, WIDE), lambda k, o: (0, o[k]))],
            out_specs=total,
        ),
        out_shape=jax.ShapeDtypeStruct((ROWS, heads), jnp.float32),
        cost_estimate=pl.CostEstimate(
            flops=2 * count * ROWS * heads * WIDE,
            bytes_accessed=count * WIDE * 2 * heads,
            transcendentals=0,
        ),
    )(order, *parts, *extra, weights)


def encode(value):
    top = jnp.maximum(jnp.max(jnp.abs(value), axis=0, keepdims=True), 1e-30)
    level = jnp.ceil(jnp.log2(top) * 256.0) + 1.0
    codes = jnp.round(value * (LEVELS * jnp.exp2(level * (-1.0 / 256.0))))
    both = jnp.concatenate([codes, jnp.broadcast_to(level, (16, value.shape[1]))], axis=0)
    return both.astype(jnp.int32).astype(jnp.int16)


def decode(coded):
    coded = coded.astype(jnp.int32).astype(jnp.float32)
    rows = coded.shape[0] - 16
    return coded[:rows] * (jnp.exp2(coded[rows : rows + 1] * (1.0 / 256.0)) * (1.0 / LEVELS))


def on_device(weights, contexts, residual, plan, upstream):
    w_local = weights[0]
    chosen = plan[0]
    context = lax.dynamic_index_in_dim(contexts[0], chosen, 0, keepdims=False)
    stream = lax.dynamic_index_in_dim(residual[0], chosen, 0, keepdims=False)

    place = lax.axis_index("tensor")
    chips = lax.axis_size("tensor") // 2
    chip, core = place // 2, place % 2
    way = 1 - 2 * core
    first = core == 0
    half = ROWS // 2

    def chunk(by):
        return (chip + way * by + 2 * chips) % chips

    def mine_half(x):
        return jnp.where(first, x[:half], x[half:])

    def other_half(x):
        return jnp.where(first, x[half:], x[:half])

    def at_half(x):
        zero = jnp.zeros_like(x)
        return jnp.where(first, jnp.concatenate([x, zero], 0), jnp.concatenate([zero, x], 0))

    same = next_section(upstream[0], -1)
    other = next_section(upstream[0], -1, flip=True)
    u0 = jnp.where(first, jnp.concatenate([same, other], 1), jnp.concatenate([other, same], 1))

    far = project(jnp.stack([chunk(-3), chunk(4), chunk(3)]).astype(jnp.int32), context, w_local, 3)
    near = project(
        jnp.stack([chunk(-2), chunk(-1), chunk(0), chunk(2), chunk(1)]).astype(jnp.int32), context, w_local, 5
    )
    far_in = core_swap(jnp.concatenate([far[0], other_half(far[1])], 0))
    own = near[2]
    own_mine = jnp.where(first, own[:, : WIDE // 2], own[:, WIDE // 2 :])
    own_other = jnp.where(first, own[:, WIDE // 2 :], own[:, : WIDE // 2])
    near_in = core_swap(jnp.concatenate([near[0], near[1]], 0))
    own_in = core_swap(own_other)

    q3 = split_shift(encode(far[2] + far_in[:ROWS]), 1)
    q4 = split_shift(encode(mine_half(far[1]) + far_in[ROWS:]), 2)
    q1 = split_shift(encode(near[4] + near_in[ROWS:]), 1)
    q2 = split_shift(encode(near[3] + near_in[:ROWS] + decode(q3) + at_half(decode(q4))), 2)

    g1 = split_shift(u0, 1)
    g2 = split_shift(u0, 2)
    g3 = split_shift(g2, 1)
    g4 = split_shift(mine_half(g2), 2)
    h12 = core_swap(jnp.concatenate([g1, g2], 0))
    h34 = core_swap(jnp.concatenate([g3, g4], 0))

    here = decode(q1) + decode(q2)
    here_mine = jnp.where(first, here[:, : WIDE // 2], here[:, WIDE // 2 :])
    here_other = jnp.where(first, here[:, WIDE // 2 :], here[:, : WIDE // 2])
    projected = own_mine + own_in + here_mine + core_swap(here_other)
    hidden = (stream.astype(jnp.float32) + projected).astype(jnp.bfloat16)
    boundary = next_section(hidden, 1)

    early = backproject(
        jnp.stack([chunk(0), chunk(-1), chunk(-2), chunk(1), chunk(2)]).astype(jnp.int32),
        [u0, g1, g2, h12[:ROWS], h12[ROWS:]],
        None,
        w_local,
    )
    facing = jnp.where(
        first, jnp.concatenate([g4, h34[ROWS:]], 0), jnp.concatenate([h34[ROWS:], g4], 0)
    )
    gradient = backproject(
        jnp.stack([chunk(-3), chunk(3), chunk(4)]).astype(jnp.int32),
        [g3, h34[:ROWS], facing],
        early,
        w_local,
    )
    return (boundary[None], gradient.astype(jnp.bfloat16)[None])


def solution(mesh):
    return jax.shard_map(
        on_device,
        mesh=mesh,
        in_specs=(
            P("section", "tensor", None),
            P("section", None, "dp", "tensor"),
            P("section", None, "dp", "tensor"),
            P("section"),
            P("section", "dp", "tensor"),
        ),
        out_specs=(P("section", "dp", "tensor"), P("section", "dp", "tensor")),
        check_vma=False,
    )
```

```python
import jax
import jax.numpy as jnp
from jax import lax
from jax.experimental import pallas as pl
from jax.experimental.pallas import tpu as pltpu
from jax.sharding import PartitionSpec as P

ROWS = 128
HALF = 64
BLOCK = 512
WIDE = 1024
LEVELS = 32700.0
F32, BF16, CODE = jnp.float32, jnp.bfloat16, jnp.int16

SMEM = pl.BlockSpec(memory_space=pltpu.SMEM)
VMEM = pl.BlockSpec(memory_space=pltpu.VMEM)
ANY = pl.BlockSpec(memory_space=pl.ANY)


def split_shift(value, by):
    peers = lax.axis_size("tensor")
    chips = peers // 2
    pairs = []
    for chip in range(chips):
        pairs.append((2 * chip, 2 * ((chip + by) % chips)))
        pairs.append((2 * chip + 1, 2 * ((chip - by) % chips) + 1))
    return lax.ppermute(value, "tensor", pairs)


def core_swap(value):
    peers = lax.axis_size("tensor")
    return lax.ppermute(value, "tensor", [(i, i ^ 1) for i in range(peers)])


def next_section(value, by, shift=0):
    sections, peers = lax.axis_size("section"), lax.axis_size("tensor")
    pairs = []
    for s in range(sections):
        for t in range(peers):
            chip = (t // 2 + (1 - 2 * (t % 2)) * shift) % (peers // 2)
            pairs.append((s * peers + t, ((s + by) % sections) * peers + 2 * chip + t % 2))
    return lax.ppermute(value, ("section", "tensor"), pairs)


def call(body, outs, ins, specs, scratch=(), flops=0, moved=0, vmem=24):
    return pl.pallas_call(
        body,
        grid=(1,),
        in_specs=specs,
        out_specs=[VMEM] * len(outs),
        out_shape=[jax.ShapeDtypeStruct(s, d) for s, d in outs],
        scratch_shapes=list(scratch),
        compiler_params=pltpu.CompilerParams(vmem_limit_bytes=vmem * 2**20),
        cost_estimate=pl.CostEstimate(flops=flops, bytes_accessed=moved, transcendentals=0),
    )(*ins)


def rows_of(count, index, width=WIDE):
    return pl.BlockSpec((count, width), lambda i: (index, 0))


def chunk_of(place, by, chips):
    core = place % 2
    return (place // 2 + (1 - 2 * core) * by + 2 * chips) % chips


def chunk_of_weights(w_ref, place, by, chips):
    return w_ref[:, pl.ds(pl.multiple_of(chunk_of(place, by, chips) * WIDE, WIDE), WIDE)]


def encode(value, out_ref):
    rows = value.shape[0]
    top = jnp.maximum(jnp.max(jnp.abs(value), axis=0, keepdims=True), 1e-30)
    level = jnp.ceil(jnp.log2(top) * 256.0) + 1.0
    codes = jnp.round(value * (LEVELS * jnp.exp2(level * (-1.0 / 256.0))))
    out_ref[:rows] = codes.astype(jnp.int32).astype(CODE)
    out_ref[rows:] = jnp.broadcast_to(level, (16, value.shape[1])).astype(jnp.int32).astype(CODE)


def decode(ref):
    rows = ref.shape[0] - 16
    level = ref[rows:].astype(jnp.int32).astype(F32)[:1]
    return ref[:rows].astype(jnp.int32).astype(F32) * (jnp.exp2(level * (1.0 / 256.0)) * (1.0 / LEVELS))


def project(place, plan, contexts, weights, chips):

    order = (-3, 3, -2, 2, -1, 1, 4, 0)

    def body(place_ref, plan_ref, ctx_ref, w_ref, send_ref, keep_ref, own_ref, held, ctx, full, sems, ctx_sem):
        here = place_ref[0]
        core = here % 2
        mine, theirs = core, 1 - core
        fetch = pltpu.make_async_copy(ctx_ref.at[plan_ref[0]], ctx, ctx_sem)
        fetch.start()
        copies = []
        for slot, by in enumerate(order):
            at = pl.multiple_of(chunk_of(here, by, chips) * WIDE, WIDE)
            copies.append(pltpu.make_async_copy(w_ref.at[:, pl.ds(at, WIDE)], held.at[slot], sems.at[slot]))
        for copy in copies:
            copy.start()
        fetch.wait()

        def product(by):
            slot = order.index(by)
            copies[slot].wait()
            return jnp.dot(ctx[...], held[slot], preferred_element_type=F32)

        for slot, by in enumerate((3, 2, 1)):
            rows = slice(slot * ROWS, (slot + 1) * ROWS)
            send_ref[rows] = product(-by)
            keep_ref[rows] = product(by)
        full[...] = product(4)
        send_ref[3 * ROWS : 3 * ROWS + HALF] = full[pl.ds(pl.multiple_of(theirs * HALF, HALF), HALF)]
        keep_ref[3 * ROWS :] = full[pl.ds(pl.multiple_of(mine * HALF, HALF), HALF)]
        full[...] = product(0)
        for part, at in ((0, 0), (1, HALF)):
            lanes = slice(part * BLOCK, (part + 1) * BLOCK)
            rows = slice(at, at + HALF)
            send_ref[3 * ROWS + HALF :, lanes] = full[rows, pl.ds(pl.multiple_of(theirs * BLOCK, BLOCK), BLOCK)]
            own_ref[:, lanes] = full[rows, pl.ds(pl.multiple_of(mine * BLOCK, BLOCK), BLOCK)]

    heads = weights.shape[0]
    return call(
        body,
        [((4 * ROWS, WIDE), F32), ((3 * ROWS + HALF, WIDE), F32), ((HALF, WIDE), F32)],
        (place, plan, contexts, weights),
        [SMEM, SMEM, ANY, ANY],
        [
            pltpu.VMEM((8, heads, WIDE), BF16),
            pltpu.VMEM((ROWS, heads), BF16),
            pltpu.VMEM((ROWS, WIDE), F32),
            pltpu.SemaphoreType.DMA((8,)),
            pltpu.SemaphoreType.DMA,
        ],
        flops=16 * ROWS * heads * WIDE,
        moved=16 * heads * WIDE,
        vmem=58,
    )


def encode_far(place, keep, arrived):
    def body(place_ref, keep_ref, in_ref, q3_ref, q4_ref, q1_ref):
        encode(keep_ref[:ROWS] + in_ref[:ROWS], q3_ref)
        encode(keep_ref[3 * ROWS :] + in_ref[3 * ROWS : 3 * ROWS + HALF], q4_ref)
        encode(keep_ref[2 * ROWS : 3 * ROWS] + in_ref[2 * ROWS : 3 * ROWS], q1_ref)

    return call(
        body,
        [((ROWS + 16, WIDE), CODE), ((HALF + 16, WIDE), CODE), ((ROWS + 16, WIDE), CODE)],
        (place, keep, arrived),
        [SMEM, VMEM, VMEM],
        flops=2**21,
        moved=2**21,
    )


def encode_two(place, keep, arrived, q3, q4):
    def body(place_ref, keep_ref, in_ref, q3_ref, q4_ref, q_ref, total):
        mine = pl.multiple_of((place_ref[0] % 2) * HALF, HALF)
        total[...] = keep_ref[...] + in_ref[...] + decode(q3_ref)
        total[pl.ds(mine, HALF)] += decode(q4_ref)
        encode(total[...], q_ref)

    return call(
        body,
        [((ROWS + 16, WIDE), CODE)],
        (place, keep, arrived, q3, q4),
        [SMEM, rows_of(ROWS, 1), rows_of(ROWS, 1), VMEM, VMEM],
        [pltpu.VMEM((ROWS, WIDE), F32)],
        flops=2**20,
        moved=2**21,
    )[0]


def gather_home(place, plan, q1, q2, own, arrived, residual):
    def body(place_ref, plan_ref, q1_ref, q2_ref, own_ref, in_ref, res_ref, send_ref, part_ref, full, stream, sem):
        fetch = pltpu.make_async_copy(res_ref.at[plan_ref[0]], stream, sem)
        fetch.start()
        core = place_ref[0] % 2
        mine = pl.multiple_of(core * BLOCK, BLOCK)
        theirs = pl.multiple_of((1 - core) * BLOCK, BLOCK)
        full[...] = decode(q1_ref) + decode(q2_ref)
        send_ref[...] = full[:, pl.ds(theirs, BLOCK)]
        fetch.wait()
        for part, at in ((0, 0), (1, HALF)):
            lanes = slice(part * BLOCK, (part + 1) * BLOCK)
            rows = slice(at, at + HALF)
            part_ref[rows] = (
                full[rows, pl.ds(mine, BLOCK)]
                + own_ref[:, lanes]
                + in_ref[:, lanes]
                + stream[rows].astype(F32)
            )

    return call(
        body,
        [((ROWS, BLOCK), F32)] * 2,
        (place, plan, q1, q2, own, arrived, residual),
        [SMEM, SMEM, VMEM, VMEM, VMEM, rows_of(HALF, 7), ANY],
        [pltpu.VMEM((ROWS, WIDE), F32), pltpu.VMEM((ROWS, BLOCK), BF16), pltpu.SemaphoreType.DMA],
        flops=2**20,
        moved=2**21,
    )


def times_transposed(x, w):
    return lax.dot_general(x, w, (((1,), (1,)), ((), ())), preferred_element_type=F32)


def backproject_first(place, parts, weights, chips):
    offsets = (0, -1, -2, -3)

    def body(place_ref, u_ref, g1_ref, g2_ref, g3_ref, w_ref, out_ref):
        for slot, x in enumerate((u_ref, g1_ref, g2_ref, g3_ref)):
            term = times_transposed(x[...], chunk_of_weights(w_ref, place_ref[0], offsets[slot], chips))
            out_ref[...] = term if slot == 0 else out_ref[...] + term

    heads = weights.shape[0]
    return call(
        body,
        [((ROWS, heads), F32)],
        (place, *parts, weights),
        [SMEM] + [VMEM] * 5,
        flops=8 * ROWS * heads * WIDE,
        moved=8 * heads * WIDE,
    )[0]


def backproject_rest(place, swapped, g4, start, weights, chips):
    offsets = (1, 2, 3, 4)

    def body(place_ref, h_ref, g4_ref, start_ref, w_ref, out_ref, facing, total):
        core = place_ref[0] % 2
        facing[pl.ds(pl.multiple_of(core * HALF, HALF), HALF)] = g4_ref[...]
        facing[pl.ds(pl.multiple_of((1 - core) * HALF, HALF), HALF)] = h_ref[3 * ROWS :]
        total[...] = start_ref[...]
        for slot in range(3):
            total[...] += times_transposed(
                h_ref[slot * ROWS : (slot + 1) * ROWS],
                chunk_of_weights(w_ref, place_ref[0], offsets[slot], chips),
            )
        last = times_transposed(facing[...], chunk_of_weights(w_ref, place_ref[0], offsets[3], chips))
        out_ref[...] = (total[...] + last).astype(BF16)

    heads = weights.shape[0]
    return call(
        body,
        [((ROWS, heads), BF16)],
        (place, swapped, g4, start, weights),
        [SMEM] + [VMEM] * 4,
        [
            pltpu.VMEM((ROWS, WIDE), BF16),
            pltpu.VMEM((ROWS, heads), F32),
        ],
        flops=8 * ROWS * heads * WIDE,
        moved=8 * heads * WIDE,
    )[0]


def on_device(weights, contexts, residual, plan, upstream):
    w_local, contexts, residual = weights[0], contexts[0], residual[0]
    at = lax.axis_index("tensor")
    place = at.astype(jnp.int32)[None]
    chips = lax.axis_size("tensor") // 2
    first = at % 2 == 0

    mate = core_swap(upstream[0])
    pair = jnp.where(
        first, jnp.concatenate([upstream[0], mate], 1), jnp.concatenate([mate, upstream[0]], 1)
    )
    g1 = next_section(pair, -1, 1)
    g2 = next_section(pair, -1, 2)
    g0 = next_section(pair, -1)

    send, keep, own = project(place, plan, contexts, w_local, chips)
    arrived = core_swap(send)
    q3, q4, q1 = encode_far(place, keep, arrived)
    g2, _ = lax.optimization_barrier((g2, q3))
    q3, q4 = split_shift(q3, 1), split_shift(q4, 2)
    q1 = split_shift(q1, 1)
    q2 = split_shift(encode_two(place, keep, arrived, q3, q4), 2)

    g3 = split_shift(g2, 1)
    g4 = split_shift(jnp.where(first, g2[:HALF], g2[HALF:]), 2)
    g1, g0 = lax.optimization_barrier((g1, g0))
    early = backproject_first(place, (g0, g1, g2, g3), w_local, chips)
    swapped = core_swap(jnp.concatenate([g1, g2, g3, g4], 0))

    after, _ = lax.optimization_barrier((place, early))
    send, part = gather_home(after, plan, q1, q2, own, arrived, residual)
    hidden = (part + core_swap(send)).astype(BF16)
    boundary = next_section(hidden, 1)
    gradient = backproject_rest(place, swapped, g4, early, w_local, chips)
    boundary, gradient = lax.optimization_barrier((boundary, gradient))
    return (boundary[None], gradient[None])


def solution(mesh):
    return jax.shard_map(
        on_device,
        mesh=mesh,
        in_specs=(
            P("section", "tensor", None),
            P("section", None, "dp", "tensor"),
            P("section", None, "dp", "tensor"),
            P("section"),
            P("section", "dp", "tensor"),
        ),
        out_specs=(P("section", "dp", "tensor"), P("section", "dp", "tensor")),
        check_vma=False,
    )
```

```python
import jax
import jax.numpy as jnp
from jax import lax
from jax.experimental import pallas as pl
from jax.experimental.pallas import tpu as pltpu
from jax.sharding import PartitionSpec as P

ROWS = 128
HALF = 64
BLOCK = 512
WIDE = 1024
LEVELS = 32700.0
F32, BF16, CODE = jnp.float32, jnp.bfloat16, jnp.int16

SMEM = pl.BlockSpec(memory_space=pltpu.SMEM)
VMEM = pl.BlockSpec(memory_space=pltpu.VMEM)
ANY = pl.BlockSpec(memory_space=pl.ANY)


def split_shift(value, by):
    peers = lax.axis_size("tensor")
    chips = peers // 2
    pairs = []
    for chip in range(chips):
        pairs.append((2 * chip, 2 * ((chip + by) % chips)))
        pairs.append((2 * chip + 1, 2 * ((chip - by) % chips) + 1))
    return lax.ppermute(value, "tensor", pairs)


def core_swap(value):
    peers = lax.axis_size("tensor")
    return lax.ppermute(value, "tensor", [(i, i ^ 1) for i in range(peers)])


def next_section(value, by, shift=0):
    sections, peers = lax.axis_size("section"), lax.axis_size("tensor")
    pairs = []
    for s in range(sections):
        for t in range(peers):
            chip = (t // 2 + (1 - 2 * (t % 2)) * shift) % (peers // 2)
            pairs.append((s * peers + t, ((s + by) % sections) * peers + 2 * chip + t % 2))
    return lax.ppermute(value, ("section", "tensor"), pairs)


def call(body, outs, ins, specs, scratch=(), vmem=24):
    return pl.pallas_call(
        body,
        grid=(1,),
        in_specs=specs,
        out_specs=[VMEM] * len(outs),
        out_shape=[jax.ShapeDtypeStruct(s, d) for s, d in outs],
        scratch_shapes=list(scratch),
        compiler_params=pltpu.CompilerParams(vmem_limit_bytes=vmem * 2**20),
        cost_estimate=pl.CostEstimate(flops=1, bytes_accessed=1, transcendentals=0),
    )(*ins)


def rows_of(count, index, width=WIDE):
    return pl.BlockSpec((count, width), lambda i: (index, 0))


def chunk_of(place, by, chips):
    core = place % 2
    return (place // 2 + (1 - 2 * core) * by + 2 * chips) % chips


def chunk_of_weights(w_ref, place, by, chips):
    return w_ref[:, pl.ds(pl.multiple_of(chunk_of(place, by, chips) * WIDE, WIDE), WIDE)]


def encode(value, out_ref):
    rows = value.shape[0]
    top = jnp.maximum(jnp.max(jnp.abs(value), axis=0, keepdims=True), 1e-30)
    level = jnp.ceil(jnp.log2(top) * 256.0) + 1.0
    codes = jnp.round(value * (LEVELS * jnp.exp2(level * (-1.0 / 256.0))))
    out_ref[:rows] = codes.astype(jnp.int32).astype(CODE)
    out_ref[rows:] = jnp.broadcast_to(level, (16, value.shape[1])).astype(jnp.int32).astype(CODE)


def decode(ref):
    rows = ref.shape[0] - 16
    level = ref[rows:].astype(jnp.int32).astype(F32)[:1]
    return ref[:rows].astype(jnp.int32).astype(F32) * (jnp.exp2(level * (1.0 / 256.0)) * (1.0 / LEVELS))


def project(place, plan, contexts, weights, chips):

    order = (-3, 3, -2, 2, -1, 1, 4, 0)

    def body(place_ref, plan_ref, ctx_ref, w_ref, send_ref, keep_ref, own_ref, held, ctx, full, sems, ctx_sem):
        here = place_ref[0]
        core = here % 2
        mine, theirs = core, 1 - core
        fetch = pltpu.make_async_copy(ctx_ref.at[plan_ref[0]], ctx, ctx_sem)
        fetch.start()
        copies = []
        for slot, by in enumerate(order):
            at = pl.multiple_of(chunk_of(here, by, chips) * WIDE, WIDE)
            copies.append(pltpu.make_async_copy(w_ref.at[:, pl.ds(at, WIDE)], held.at[slot], sems.at[slot]))
        for copy in copies:
            copy.start()
        fetch.wait()

        def product(by):
            slot = order.index(by)
            copies[slot].wait()
            return jnp.dot(ctx[...], held[slot], preferred_element_type=F32)

        for slot, by in enumerate((3, 2, 1)):
            rows = slice(slot * ROWS, (slot + 1) * ROWS)
            send_ref[rows] = product(-by)
            keep_ref[rows] = product(by)
        full[...] = product(4)
        send_ref[3 * ROWS : 3 * ROWS + HALF] = full[pl.ds(pl.multiple_of(theirs * HALF, HALF), HALF)]
        keep_ref[3 * ROWS :] = full[pl.ds(pl.multiple_of(mine * HALF, HALF), HALF)]
        full[...] = product(0)
        for part, at in ((0, 0), (1, HALF)):
            lanes = slice(part * BLOCK, (part + 1) * BLOCK)
            rows = slice(at, at + HALF)
            send_ref[3 * ROWS + HALF :, lanes] = full[rows, pl.ds(pl.multiple_of(theirs * BLOCK, BLOCK), BLOCK)]
            own_ref[:, lanes] = full[rows, pl.ds(pl.multiple_of(mine * BLOCK, BLOCK), BLOCK)]

    heads = weights.shape[0]
    return call(
        body,
        [((4 * ROWS, WIDE), F32), ((3 * ROWS + HALF, WIDE), F32), ((HALF, WIDE), F32)],
        (place, plan, contexts, weights),
        [SMEM, SMEM, ANY, ANY],
        [
            pltpu.VMEM((8, heads, WIDE), BF16),
            pltpu.VMEM((ROWS, heads), BF16),
            pltpu.VMEM((ROWS, WIDE), F32),
            pltpu.SemaphoreType.DMA((8,)),
            pltpu.SemaphoreType.DMA,
        ],
        vmem=46,
    )


def encode_first(place, keep, arrived):
    def body(place_ref, keep_ref, in_ref, q31_ref, q4_ref):
        coded = ROWS + 16
        encode(keep_ref[:ROWS] + in_ref[:ROWS], q31_ref.at[:coded])
        encode(keep_ref[2 * ROWS : 3 * ROWS] + in_ref[2 * ROWS : 3 * ROWS], q31_ref.at[coded:])
        encode(keep_ref[3 * ROWS :] + in_ref[3 * ROWS : 3 * ROWS + HALF], q4_ref)

    return call(
        body,
        [((2 * ROWS + 32, WIDE), CODE), ((HALF + 16, WIDE), CODE)],
        (place, keep, arrived),
        [SMEM, VMEM, VMEM],
    )


def encode_two(keep, arrived, q31):
    def body(keep_ref, in_ref, q3_ref, q_ref):
        encode(keep_ref[...] + in_ref[...] + decode(q3_ref), q_ref)

    return call(
        body,
        [((ROWS + 16, WIDE), CODE)],
        (keep, arrived, q31),
        [rows_of(ROWS, 1), rows_of(ROWS, 1), rows_of(ROWS + 16, 0)],
    )[0]


def gather_home(place, plan, q31, q2, q4, own, arrived, residual):
    def body(place_ref, plan_ref, q1_ref, q2_ref, q4_ref, own_ref, in_ref, res_ref, send_ref, part_ref, full, stream, sem):
        fetch = pltpu.make_async_copy(res_ref.at[plan_ref[0]], stream, sem)
        fetch.start()
        core = place_ref[0] % 2
        mine = pl.multiple_of(core * BLOCK, BLOCK)
        theirs = pl.multiple_of((1 - core) * BLOCK, BLOCK)
        full[...] = decode(q1_ref) + decode(q2_ref)
        full[pl.ds(pl.multiple_of(core * HALF, HALF), HALF)] += decode(q4_ref)
        send_ref[...] = full[:, pl.ds(theirs, BLOCK)]
        fetch.wait()
        for part, at in ((0, 0), (1, HALF)):
            lanes = slice(part * BLOCK, (part + 1) * BLOCK)
            rows = slice(at, at + HALF)
            part_ref[rows] = (
                full[rows, pl.ds(mine, BLOCK)]
                + own_ref[:, lanes]
                + in_ref[:, lanes]
                + stream[rows].astype(F32)
            )

    return call(
        body,
        [((ROWS, BLOCK), F32)] * 2,
        (place, plan, q31, q2, q4, own, arrived, residual),
        [SMEM, SMEM, rows_of(ROWS + 16, 1), VMEM, VMEM, VMEM, rows_of(HALF, 7), ANY],
        [pltpu.VMEM((ROWS, WIDE), F32), pltpu.VMEM((ROWS, BLOCK), BF16), pltpu.SemaphoreType.DMA],
    )


def times_transposed(x, w):
    return lax.dot_general(x, w, (((1,), (1,)), ((), ())), preferred_element_type=F32)


def backproject_first(place, parts, weights, chips):
    offsets = (0, -1, -2)

    def body(place_ref, u_ref, g1_ref, g2_ref, w_ref, out_ref):
        for slot, x in enumerate((u_ref, g1_ref, g2_ref)):
            term = times_transposed(x[...], chunk_of_weights(w_ref, place_ref[0], offsets[slot], chips))
            out_ref[...] = term if slot == 0 else out_ref[...] + term

    heads = weights.shape[0]
    return call(
        body,
        [((ROWS, heads), F32)],
        (place, *parts, weights),
        [SMEM] + [VMEM] * 4,
    )[0]


def backproject_rest(place, h1, h2, h34, g3, g4, start, weights, chips):
    offsets = (1, 2, 3, -3, 4)

    def body(place_ref, h1_ref, h2_ref, h34_ref, g3_ref, g4_ref, start_ref, w_ref, out_ref, facing, total):
        core = place_ref[0] % 2
        facing[pl.ds(pl.multiple_of(core * HALF, HALF), HALF)] = g4_ref[...]
        facing[pl.ds(pl.multiple_of((1 - core) * HALF, HALF), HALF)] = h34_ref[ROWS:]
        total[...] = start_ref[...]
        for slot, x in enumerate((h1_ref, h2_ref, h34_ref.at[:ROWS], g3_ref)):
            total[...] += times_transposed(x[...], chunk_of_weights(w_ref, place_ref[0], offsets[slot], chips))
        last = times_transposed(facing[...], chunk_of_weights(w_ref, place_ref[0], offsets[4], chips))
        out_ref[...] = (total[...] + last).astype(BF16)

    heads = weights.shape[0]
    return call(
        body,
        [((ROWS, heads), BF16)],
        (place, h1, h2, h34, g3, g4, start, weights),
        [SMEM] + [VMEM] * 7,
        [
            pltpu.VMEM((ROWS, WIDE), BF16),
            pltpu.VMEM((ROWS, heads), F32),
        ],
    )[0]


def on_device(weights, contexts, residual, plan, upstream):
    w_local, contexts, residual = weights[0], contexts[0], residual[0]
    at = lax.axis_index("tensor")
    place = at.astype(jnp.int32)[None]
    chips = lax.axis_size("tensor") // 2
    first = at % 2 == 0

    send, keep, own = project(place, plan, contexts, w_local, chips)
    arrived = core_swap(send)
    mate = core_swap(upstream[0])
    pair = jnp.where(
        first, jnp.concatenate([upstream[0], mate], 1), jnp.concatenate([mate, upstream[0]], 1)
    )
    after, pair = lax.optimization_barrier((place, pair))
    q31, q4 = encode_first(after, keep, arrived)
    q31, q4 = split_shift(q31, 1), split_shift(q4, 4)
    q2 = split_shift(encode_two(keep, arrived, q31), 2)

    g1 = next_section(pair, -1, 1)
    g2 = next_section(pair, -1, 2)
    g3 = split_shift(g2, 1)
    g4 = split_shift(jnp.where(first, g2[:HALF], g2[HALF:]), 2)
    g0 = next_section(pair, -1)
    to_mate, q4 = lax.optimization_barrier((g1, q4))
    h1 = core_swap(to_mate)
    to_mate, g0 = lax.optimization_barrier((g2, g0))
    h2 = core_swap(to_mate)
    h34 = core_swap(jnp.concatenate([g3, g4], 0))
    early = backproject_first(place, (g0, g1, g2), w_local, chips)

    after, _, _, _ = lax.optimization_barrier((place, early, h1, h2))
    send, part = gather_home(after, plan, q31, q2, q4, own, arrived, residual)
    hidden = (part + core_swap(send)).astype(BF16)
    boundary = next_section(hidden, 1)
    gradient = backproject_rest(place, h1, h2, h34, g3, g4, early, w_local, chips)
    boundary, gradient = lax.optimization_barrier((boundary, gradient))
    return (boundary[None], gradient[None])


def solution(mesh):
    return jax.shard_map(
        on_device,
        mesh=mesh,
        in_specs=(
            P("section", "tensor", None),
            P("section", None, "dp", "tensor"),
            P("section", None, "dp", "tensor"),
            P("section"),
            P("section", "dp", "tensor"),
        ),
        out_specs=(P("section", "dp", "tensor"), P("section", "dp", "tensor")),
        check_vma=False,
    )
```

```python
import jax
import jax.numpy as jnp
from jax import lax
from jax.experimental import pallas as pl
from jax.experimental.pallas import tpu as pltpu
from jax.sharding import PartitionSpec as P

ROWS = 128
HALF = 64
BLOCK = 512
WIDE = 1024
LEVELS = 32700.0
F32, BF16, CODE = jnp.float32, jnp.bfloat16, jnp.int16

SMEM = pl.BlockSpec(memory_space=pltpu.SMEM)
VMEM = pl.BlockSpec(memory_space=pltpu.VMEM)
ANY = pl.BlockSpec(memory_space=pl.ANY)


def split_shift(value, by):
    peers = lax.axis_size("tensor")
    chips = peers // 2
    pairs = []
    for chip in range(chips):
        pairs.append((2 * chip, 2 * ((chip + by) % chips)))
        pairs.append((2 * chip + 1, 2 * ((chip - by) % chips) + 1))
    return lax.ppermute(value, "tensor", pairs)


def core_swap(value):
    peers = lax.axis_size("tensor")
    return lax.ppermute(value, "tensor", [(i, i ^ 1) for i in range(peers)])


def next_section(value, by, shift=0):
    sections, peers = lax.axis_size("section"), lax.axis_size("tensor")
    pairs = []
    for s in range(sections):
        for t in range(peers):
            chip = (t // 2 + (1 - 2 * (t % 2)) * shift) % (peers // 2)
            pairs.append((s * peers + t, ((s + by) % sections) * peers + 2 * chip + t % 2))
    return lax.ppermute(value, ("section", "tensor"), pairs)


def call(body, outs, ins, specs, scratch=(), vmem=24):
    return pl.pallas_call(
        body,
        grid=(1,),
        in_specs=specs,
        out_specs=[VMEM] * len(outs),
        out_shape=[jax.ShapeDtypeStruct(s, d) for s, d in outs],
        scratch_shapes=list(scratch),
        compiler_params=pltpu.CompilerParams(vmem_limit_bytes=vmem * 2**20),
        cost_estimate=pl.CostEstimate(flops=1, bytes_accessed=1, transcendentals=0),
    )(*ins)


def rows_of(count, index, width=WIDE):
    return pl.BlockSpec((count, width), lambda i: (index, 0))


def chunk_of(place, by, chips):
    core = place % 2
    return (place // 2 + (1 - 2 * core) * by + 2 * chips) % chips


def chunk_of_weights(w_ref, place, by, chips):
    return w_ref[:, pl.ds(pl.multiple_of(chunk_of(place, by, chips) * WIDE, WIDE), WIDE)]


def encode(value, out_ref):
    rows = value.shape[0]
    top = jnp.maximum(jnp.max(jnp.abs(value), axis=0, keepdims=True), 1e-30)
    level = jnp.ceil(jnp.log2(top) * 256.0) + 1.0
    codes = jnp.round(value * (LEVELS * jnp.exp2(level * (-1.0 / 256.0))))
    out_ref[:rows] = codes.astype(jnp.int32).astype(CODE)
    out_ref[rows:] = jnp.broadcast_to(level, (16, value.shape[1])).astype(jnp.int32).astype(CODE)


def decode(ref):
    rows = ref.shape[0] - 16
    level = ref[rows:].astype(jnp.int32).astype(F32)[:1]
    return ref[:rows].astype(jnp.int32).astype(F32) * (jnp.exp2(level * (1.0 / 256.0)) * (1.0 / LEVELS))


def project(place, plan, contexts, weights, chips):

    order = (-3, 3, -2, 2, -1, 1, 4, 0)

    def body(place_ref, plan_ref, ctx_ref, w_ref, send_ref, keep3_ref, keep2_ref, keep1_ref, keep4_ref, own_ref, held, ctx, full, sems, ctx_sem):
        here = place_ref[0]
        core = here % 2
        mine, theirs = core, 1 - core
        fetch = pltpu.make_async_copy(ctx_ref.at[plan_ref[0]], ctx, ctx_sem)
        fetch.start()
        copies = []
        for slot, by in enumerate(order):
            at = pl.multiple_of(chunk_of(here, by, chips) * WIDE, WIDE)
            copies.append(pltpu.make_async_copy(w_ref.at[:, pl.ds(at, WIDE)], held.at[slot], sems.at[slot]))
        for copy in copies:
            copy.start()
        fetch.wait()

        def product(by):
            slot = order.index(by)
            copies[slot].wait()
            return jnp.dot(ctx[...], held[slot], preferred_element_type=F32)

        for slot, (by, keep_ref) in enumerate(((3, keep3_ref), (2, keep2_ref), (1, keep1_ref))):
            send_ref[slot * ROWS : (slot + 1) * ROWS] = product(-by)
            keep_ref[...] = product(by)
        full[...] = product(4)
        send_ref[3 * ROWS : 3 * ROWS + HALF] = full[pl.ds(pl.multiple_of(theirs * HALF, HALF), HALF)]
        keep4_ref[...] = full[pl.ds(pl.multiple_of(mine * HALF, HALF), HALF)]
        full[...] = product(0)
        for part, at in ((0, 0), (1, HALF)):
            lanes = slice(part * BLOCK, (part + 1) * BLOCK)
            rows = slice(at, at + HALF)
            send_ref[3 * ROWS + HALF :, lanes] = full[rows, pl.ds(pl.multiple_of(theirs * BLOCK, BLOCK), BLOCK)]
            own_ref[:, lanes] = full[rows, pl.ds(pl.multiple_of(mine * BLOCK, BLOCK), BLOCK)]

    heads = weights.shape[0]
    return call(
        body,
        [((4 * ROWS, WIDE), F32)] + [((ROWS, WIDE), F32)] * 3 + [((HALF, WIDE), F32)] * 2,
        (place, plan, contexts, weights),
        [SMEM, SMEM, ANY, ANY],
        [
            pltpu.VMEM((8, heads, WIDE), BF16),
            pltpu.VMEM((ROWS, heads), BF16),
            pltpu.VMEM((ROWS, WIDE), F32),
            pltpu.SemaphoreType.DMA((8,)),
            pltpu.SemaphoreType.DMA,
        ],
        vmem=46,
    )


def encode_first(place, keep3, keep4, arrived):
    def body(place_ref, keep3_ref, keep4_ref, in3_ref, in4_ref, q_ref):
        encode(keep3_ref[...] + in3_ref[...], q_ref.at[: ROWS + 16])
        encode(keep4_ref[...] + in4_ref[...], q_ref.at[ROWS + 16 :])

    return call(
        body,
        [((ROWS + HALF + 32, WIDE), CODE)],
        (place, keep3, keep4, arrived, arrived),
        [SMEM, VMEM, VMEM, rows_of(ROWS, 0), rows_of(HALF, 6)],
    )[0]


def encode_two(place, keep2, keep1, arrived, q34):
    def body(place_ref, keep2_ref, keep1_ref, in2_ref, in1_ref, q34_ref, q2_ref, q1_ref, total):
        mine = pl.multiple_of((place_ref[0] % 2) * HALF, HALF)
        total[...] = keep2_ref[...] + in2_ref[...]
        total[pl.ds(mine, HALF)] += decode(q34_ref.at[ROWS + 16 :])
        encode(total[...], q2_ref)
        encode(keep1_ref[...] + in1_ref[...] + decode(q34_ref.at[: ROWS + 16]), q1_ref)

    return call(
        body,
        [((ROWS + 16, WIDE), CODE)] * 2,
        (place, keep2, keep1, arrived, arrived, q34),
        [SMEM, VMEM, VMEM, rows_of(ROWS, 1), rows_of(ROWS, 2), VMEM],
        [pltpu.VMEM((ROWS, WIDE), F32)],
    )


def gather_home(place, plan, q1, q2, own, arrived, residual):
    def body(place_ref, plan_ref, q1_ref, q2_ref, own_ref, in_ref, res_ref, send_ref, part_ref, full, stream, sem):
        fetch = pltpu.make_async_copy(res_ref.at[plan_ref[0]], stream, sem)
        fetch.start()
        core = place_ref[0] % 2
        mine = pl.multiple_of(core * BLOCK, BLOCK)
        theirs = pl.multiple_of((1 - core) * BLOCK, BLOCK)
        full[...] = decode(q1_ref) + decode(q2_ref)
        send_ref[...] = full[:, pl.ds(theirs, BLOCK)]
        fetch.wait()
        for part, at in ((0, 0), (1, HALF)):
            lanes = slice(part * BLOCK, (part + 1) * BLOCK)
            rows = slice(at, at + HALF)
            part_ref[rows] = (
                full[rows, pl.ds(mine, BLOCK)]
                + own_ref[:, lanes]
                + in_ref[:, lanes]
                + stream[rows].astype(F32)
            )

    return call(
        body,
        [((ROWS, BLOCK), F32)] * 2,
        (place, plan, q1, q2, own, arrived, residual),
        [SMEM, SMEM, VMEM, VMEM, VMEM, rows_of(HALF, 7), ANY],
        [pltpu.VMEM((ROWS, WIDE), F32), pltpu.VMEM((ROWS, BLOCK), BF16), pltpu.SemaphoreType.DMA],
    )


def times_transposed(x, w):
    return lax.dot_general(x, w, (((1,), (1,)), ((), ())), preferred_element_type=F32)


def backproject_first(place, parts, weights, chips):
    offsets = (0, -1, -2)

    def body(place_ref, u_ref, g1_ref, g2_ref, w_ref, out_ref):
        for slot, x in enumerate((u_ref, g1_ref, g2_ref)):
            term = times_transposed(x[...], chunk_of_weights(w_ref, place_ref[0], offsets[slot], chips))
            out_ref[...] = term if slot == 0 else out_ref[...] + term

    heads = weights.shape[0]
    return call(
        body,
        [((ROWS, heads), F32)],
        (place, *parts, weights),
        [SMEM] + [VMEM] * 4,
    )[0]


def backproject_rest(place, h1, h2, h34, g3, g4, start, weights, chips):
    offsets = (1, 2, 3, -3, 4)

    def body(place_ref, h1_ref, h2_ref, h34_ref, g3_ref, g4_ref, start_ref, w_ref, out_ref, facing, total):
        core = place_ref[0] % 2
        facing[pl.ds(pl.multiple_of(core * HALF, HALF), HALF)] = g4_ref[...]
        facing[pl.ds(pl.multiple_of((1 - core) * HALF, HALF), HALF)] = h34_ref[ROWS:]
        total[...] = start_ref[...]
        for slot, x in enumerate((h1_ref, h2_ref, h34_ref.at[:ROWS], g3_ref)):
            total[...] += times_transposed(x[...], chunk_of_weights(w_ref, place_ref[0], offsets[slot], chips))
        last = times_transposed(facing[...], chunk_of_weights(w_ref, place_ref[0], offsets[4], chips))
        out_ref[...] = (total[...] + last).astype(BF16)

    heads = weights.shape[0]
    return call(
        body,
        [((ROWS, heads), BF16)],
        (place, h1, h2, h34, g3, g4, start, weights),
        [SMEM] + [VMEM] * 7,
        [
            pltpu.VMEM((ROWS, WIDE), BF16),
            pltpu.VMEM((ROWS, heads), F32),
        ],
    )[0]


def on_device(weights, contexts, residual, plan, upstream):
    w_local, contexts, residual = weights[0], contexts[0], residual[0]
    at = lax.axis_index("tensor")
    place = at.astype(jnp.int32)[None]
    chips = lax.axis_size("tensor") // 2
    first = at % 2 == 0

    send, keep3, keep2, keep1, keep4, own = project(place, plan, contexts, w_local, chips)
    arrived = core_swap(send)
    mate = core_swap(upstream[0])
    pair = jnp.where(
        first, jnp.concatenate([upstream[0], mate], 1), jnp.concatenate([mate, upstream[0]], 1)
    )
    after, pair = lax.optimization_barrier((place, pair))
    q34 = split_shift(encode_first(after, keep3, keep4, arrived), 2)
    q2, q1 = encode_two(place, keep2, keep1, arrived, q34)
    q2, q1 = split_shift(q2, 2), split_shift(q1, 1)

    g1 = next_section(pair, -1, 1)
    g2 = next_section(pair, -1, 2)
    g3 = split_shift(g2, 1)
    g4 = split_shift(jnp.where(first, g2[:HALF], g2[HALF:]), 2)
    g0 = next_section(pair, -1)
    h2 = core_swap(g2)
    to_mate, g0 = lax.optimization_barrier((g1, g0))
    h1 = core_swap(to_mate)
    h34 = core_swap(jnp.concatenate([g3, g4], 0))
    early = backproject_first(place, (g0, g1, g2), w_local, chips)

    after, _, _, _ = lax.optimization_barrier((place, early, h1, h2))
    send, part = gather_home(after, plan, q1, q2, own, arrived, residual)
    hidden = (part + core_swap(send)).astype(BF16)
    boundary = next_section(hidden, 1)
    gradient = backproject_rest(place, h1, h2, h34, g3, g4, early, w_local, chips)
    boundary, gradient = lax.optimization_barrier((boundary, gradient))
    return (boundary[None], gradient[None])


def solution(mesh):
    return jax.shard_map(
        on_device,
        mesh=mesh,
        in_specs=(
            P("section", "tensor", None),
            P("section", None, "dp", "tensor"),
            P("section", None, "dp", "tensor"),
            P("section"),
            P("section", "dp", "tensor"),
        ),
        out_specs=(P("section", "dp", "tensor"), P("section", "dp", "tensor")),
        check_vma=False,
    )
```

```python
import jax
import jax.numpy as jnp
from jax import lax
from jax.experimental import pallas as pl
from jax.experimental.pallas import tpu as pltpu
from jax.sharding import PartitionSpec as P

ROWS = 128
HALF = 64
BLOCK = 512
WIDE = 1024
LEVELS = 32700.0
F32, BF16, CODE = jnp.float32, jnp.bfloat16, jnp.int16

SMEM = pl.BlockSpec(memory_space=pltpu.SMEM)
VMEM = pl.BlockSpec(memory_space=pltpu.VMEM)
ANY = pl.BlockSpec(memory_space=pl.ANY)


def split_shift(value, by):
    peers = lax.axis_size("tensor")
    chips = peers // 2
    pairs = []
    for chip in range(chips):
        pairs.append((2 * chip, 2 * ((chip + by) % chips)))
        pairs.append((2 * chip + 1, 2 * ((chip - by) % chips) + 1))
    return lax.ppermute(value, "tensor", pairs)


def core_swap(value):
    peers = lax.axis_size("tensor")
    return lax.ppermute(value, "tensor", [(i, i ^ 1) for i in range(peers)])


def next_section(value, by, shift=0):
    sections, peers = lax.axis_size("section"), lax.axis_size("tensor")
    pairs = []
    for s in range(sections):
        for t in range(peers):
            chip = (t // 2 + (1 - 2 * (t % 2)) * shift) % (peers // 2)
            pairs.append((s * peers + t, ((s + by) % sections) * peers + 2 * chip + t % 2))
    return lax.ppermute(value, ("section", "tensor"), pairs)


def call(body, outs, ins, specs, scratch=(), vmem=24):
    return pl.pallas_call(
        body,
        grid=(1,),
        in_specs=specs,
        out_specs=[VMEM] * len(outs),
        out_shape=[jax.ShapeDtypeStruct(s, d) for s, d in outs],
        scratch_shapes=list(scratch),
        compiler_params=pltpu.CompilerParams(vmem_limit_bytes=vmem * 2**20),
        cost_estimate=pl.CostEstimate(flops=1, bytes_accessed=1, transcendentals=0),
    )(*ins)


def rows_of(count, index, width=WIDE):
    return pl.BlockSpec((count, width), lambda i: (index, 0))


def chunk_of(place, by, chips):
    core = place % 2
    return (place // 2 + (1 - 2 * core) * by + 2 * chips) % chips


def chunk_of_weights(w_ref, place, by, chips):
    return w_ref[:, pl.ds(pl.multiple_of(chunk_of(place, by, chips) * WIDE, WIDE), WIDE)]


def encode(value, out_ref):
    rows = value.shape[0]
    top = jnp.maximum(jnp.max(jnp.abs(value), axis=0, keepdims=True), 1e-30)
    level = jnp.ceil(jnp.log2(top) * 256.0) + 1.0
    codes = jnp.round(value * (LEVELS * jnp.exp2(level * (-1.0 / 256.0))))
    out_ref[:rows] = codes.astype(jnp.int32).astype(CODE)
    out_ref[rows:] = jnp.broadcast_to(level, (16, value.shape[1])).astype(jnp.int32).astype(CODE)


def decode(ref):
    rows = ref.shape[0] - 16
    level = ref[rows:].astype(jnp.int32).astype(F32)[:1]
    return ref[:rows].astype(jnp.int32).astype(F32) * (jnp.exp2(level * (1.0 / 256.0)) * (1.0 / LEVELS))


def project(place, plan, contexts, weights, chips):

    order = (-3, 3, -2, 2, -1, 1, 4, 0)

    def body(place_ref, plan_ref, ctx_ref, w_ref, send_ref, keep3_ref, keep2_ref, keep1_ref, keep4_ref, own_ref, held, ctx, full, sems, ctx_sem):
        here = place_ref[0]
        core = here % 2
        mine, theirs = core, 1 - core
        fetch = pltpu.make_async_copy(ctx_ref.at[plan_ref[0]], ctx, ctx_sem)
        fetch.start()
        copies = []
        for slot, by in enumerate(order):
            at = pl.multiple_of(chunk_of(here, by, chips) * WIDE, WIDE)
            copies.append(pltpu.make_async_copy(w_ref.at[:, pl.ds(at, WIDE)], held.at[slot], sems.at[slot]))
        for copy in copies:
            copy.start()
        fetch.wait()

        def product(by):
            slot = order.index(by)
            copies[slot].wait()
            return jnp.dot(ctx[...], held[slot], preferred_element_type=F32)

        for slot, (by, keep_ref) in enumerate(((3, keep3_ref), (2, keep2_ref), (1, keep1_ref))):
            send_ref[slot * ROWS : (slot + 1) * ROWS] = product(-by)
            keep_ref[...] = product(by)
        full[...] = product(4)
        send_ref[3 * ROWS : 3 * ROWS + HALF] = full[pl.ds(pl.multiple_of(theirs * HALF, HALF), HALF)]
        keep4_ref[...] = full[pl.ds(pl.multiple_of(mine * HALF, HALF), HALF)]
        full[...] = product(0)
        for part, at in ((0, 0), (1, HALF)):
            lanes = slice(part * BLOCK, (part + 1) * BLOCK)
            rows = slice(at, at + HALF)
            send_ref[3 * ROWS + HALF :, lanes] = full[rows, pl.ds(pl.multiple_of(theirs * BLOCK, BLOCK), BLOCK)]
            own_ref[:, lanes] = full[rows, pl.ds(pl.multiple_of(mine * BLOCK, BLOCK), BLOCK)]

    heads = weights.shape[0]
    return call(
        body,
        [((4 * ROWS, WIDE), F32)] + [((ROWS, WIDE), F32)] * 3 + [((HALF, WIDE), F32)] * 2,
        (place, plan, contexts, weights),
        [SMEM, SMEM, ANY, ANY],
        [
            pltpu.VMEM((8, heads, WIDE), BF16),
            pltpu.VMEM((ROWS, heads), BF16),
            pltpu.VMEM((ROWS, WIDE), F32),
            pltpu.SemaphoreType.DMA((8,)),
            pltpu.SemaphoreType.DMA,
        ],
        vmem=46,
    )


def encode_first(place, keep3, keep4, arrived):
    def body(place_ref, keep3_ref, keep4_ref, in3_ref, in4_ref, q_ref):
        encode(keep3_ref[...] + in3_ref[...], q_ref.at[: ROWS + 16])
        encode(keep4_ref[...] + in4_ref[...], q_ref.at[ROWS + 16 :])

    return call(
        body,
        [((ROWS + HALF + 32, WIDE), CODE)],
        (place, keep3, keep4, arrived, arrived),
        [SMEM, VMEM, VMEM, rows_of(ROWS, 0), rows_of(HALF, 6)],
    )[0]


def encode_two(place, keep2, keep1, arrived, q34):
    def body(place_ref, keep2_ref, keep1_ref, in2_ref, in1_ref, q34_ref, q2_ref, q1_ref, total):
        mine = pl.multiple_of((place_ref[0] % 2) * HALF, HALF)
        total[...] = keep2_ref[...] + in2_ref[...]
        total[pl.ds(mine, HALF)] += decode(q34_ref.at[ROWS + 16 :])
        encode(total[...], q2_ref)
        encode(keep1_ref[...] + in1_ref[...] + decode(q34_ref.at[: ROWS + 16]), q1_ref)

    return call(
        body,
        [((ROWS + 16, WIDE), CODE)] * 2,
        (place, keep2, keep1, arrived, arrived, q34),
        [SMEM, VMEM, VMEM, rows_of(ROWS, 1), rows_of(ROWS, 2), VMEM],
        [pltpu.VMEM((ROWS, WIDE), F32)],
    )


def gather_home(place, plan, q1, q2, own, arrived, residual):
    def body(place_ref, plan_ref, q1_ref, q2_ref, own_ref, in_ref, res_ref, send_ref, part_ref, full, stream, sem):
        fetch = pltpu.make_async_copy(res_ref.at[plan_ref[0]], stream, sem)
        fetch.start()
        core = place_ref[0] % 2
        mine = pl.multiple_of(core * BLOCK, BLOCK)
        theirs = pl.multiple_of((1 - core) * BLOCK, BLOCK)
        full[...] = decode(q1_ref) + decode(q2_ref)
        send_ref[...] = full[:, pl.ds(theirs, BLOCK)]
        fetch.wait()
        for part, at in ((0, 0), (1, HALF)):
            lanes = slice(part * BLOCK, (part + 1) * BLOCK)
            rows = slice(at, at + HALF)
            part_ref[rows] = (
                full[rows, pl.ds(mine, BLOCK)]
                + own_ref[:, lanes]
                + in_ref[:, lanes]
                + stream[rows].astype(F32)
            )

    return call(
        body,
        [((ROWS, BLOCK), F32)] * 2,
        (place, plan, q1, q2, own, arrived, residual),
        [SMEM, SMEM, VMEM, VMEM, VMEM, rows_of(HALF, 7), ANY],
        [pltpu.VMEM((ROWS, WIDE), F32), pltpu.VMEM((ROWS, BLOCK), BF16), pltpu.SemaphoreType.DMA],
    )


def times_transposed(x, w):
    return lax.dot_general(x, w, (((1,), (1,)), ((), ())), preferred_element_type=F32)


def backproject_first(place, parts, weights, chips):
    offsets = (0, -1, -2)

    def body(place_ref, u_ref, g1_ref, g2_ref, w_ref, out_ref):
        for slot, x in enumerate((u_ref, g1_ref, g2_ref)):
            term = times_transposed(x[...], chunk_of_weights(w_ref, place_ref[0], offsets[slot], chips))
            out_ref[...] = term if slot == 0 else out_ref[...] + term

    heads = weights.shape[0]
    return call(
        body,
        [((ROWS, heads), F32)],
        (place, *parts, weights),
        [SMEM] + [VMEM] * 4,
    )[0]


def backproject_rest(place, h12, h34, g3, g4, start, weights, chips):
    offsets = (1, 2, 3, -3, 4)

    def body(place_ref, h12_ref, h34_ref, g3_ref, g4_ref, start_ref, w_ref, out_ref, facing, total):
        core = place_ref[0] % 2
        facing[pl.ds(pl.multiple_of(core * HALF, HALF), HALF)] = g4_ref[...]
        facing[pl.ds(pl.multiple_of((1 - core) * HALF, HALF), HALF)] = h34_ref[ROWS:]
        total[...] = start_ref[...]
        for slot, x in enumerate((h12_ref.at[:ROWS], h12_ref.at[ROWS:], h34_ref.at[:ROWS], g3_ref)):
            total[...] += times_transposed(x[...], chunk_of_weights(w_ref, place_ref[0], offsets[slot], chips))
        last = times_transposed(facing[...], chunk_of_weights(w_ref, place_ref[0], offsets[4], chips))
        out_ref[...] = (total[...] + last).astype(BF16)

    heads = weights.shape[0]
    return call(
        body,
        [((ROWS, heads), BF16)],
        (place, h12, h34, g3, g4, start, weights),
        [SMEM] + [VMEM] * 6,
        [
            pltpu.VMEM((ROWS, WIDE), BF16),
            pltpu.VMEM((ROWS, heads), F32),
        ],
    )[0]


def on_device(weights, contexts, residual, plan, upstream):
    w_local, contexts, residual = weights[0], contexts[0], residual[0]
    at = lax.axis_index("tensor")
    place = at.astype(jnp.int32)[None]
    chips = lax.axis_size("tensor") // 2
    first = at % 2 == 0

    mate = core_swap(upstream[0])
    pair = jnp.where(
        first, jnp.concatenate([upstream[0], mate], 1), jnp.concatenate([mate, upstream[0]], 1)
    )

    begun, pair = lax.optimization_barrier((place, pair))
    send, keep3, keep2, keep1, keep4, own = project(begun, plan, contexts, w_local, chips)
    arrived = core_swap(send)
    q34 = split_shift(encode_first(place, keep3, keep4, arrived), 2)
    q2, q1 = encode_two(place, keep2, keep1, arrived, q34)
    q2, q1 = split_shift(q2, 2), split_shift(q1, 1)

    g1 = next_section(pair, -1, 1)
    g2 = next_section(pair, -1, 2)
    g3 = split_shift(g2, 1)
    g4 = split_shift(jnp.where(first, g2[:HALF], g2[HALF:]), 2)
    g0 = next_section(pair, -1)
    h12 = core_swap(jnp.concatenate([g1, g2], 0))
    h34 = core_swap(jnp.concatenate([g3, g4], 0))
    early = backproject_first(place, (g0, g1, g2), w_local, chips)

    after, _, _ = lax.optimization_barrier((place, early, h12))
    send, part = gather_home(after, plan, q1, q2, own, arrived, residual)
    hidden = (part + core_swap(send)).astype(BF16)
    boundary = next_section(hidden, 1)
    gradient = backproject_rest(place, h12, h34, g3, g4, early, w_local, chips)
    boundary, gradient = lax.optimization_barrier((boundary, gradient))
    return (boundary[None], gradient[None])


def solution(mesh):
    return jax.shard_map(
        on_device,
        mesh=mesh,
        in_specs=(
            P("section", "tensor", None),
            P("section", None, "dp", "tensor"),
            P("section", None, "dp", "tensor"),
            P("section"),
            P("section", "dp", "tensor"),
        ),
        out_specs=(P("section", "dp", "tensor"), P("section", "dp", "tensor")),
        check_vma=False,
    )
```

```python
import jax
import jax.numpy as jnp
from jax import lax
from jax.experimental import pallas as pl
from jax.experimental.pallas import tpu as pltpu
from jax.sharding import PartitionSpec as P

ROWS = 128
HALF = 64
BLOCK = 512
WIDE = 1024
LEVELS = 32700.0
F32, BF16, CODE = jnp.float32, jnp.bfloat16, jnp.int16

SMEM = pl.BlockSpec(memory_space=pltpu.SMEM)
VMEM = pl.BlockSpec(memory_space=pltpu.VMEM)
ANY = pl.BlockSpec(memory_space=pl.ANY)


def split_shift(value, by):
    peers = lax.axis_size("tensor")
    chips = peers // 2
    pairs = []
    for chip in range(chips):
        pairs.append((2 * chip, 2 * ((chip + by) % chips)))
        pairs.append((2 * chip + 1, 2 * ((chip - by) % chips) + 1))
    return lax.ppermute(value, "tensor", pairs)


def core_swap(value):
    peers = lax.axis_size("tensor")
    return lax.ppermute(value, "tensor", [(i, i ^ 1) for i in range(peers)])


def next_section(value, by, shift=0):
    sections, peers = lax.axis_size("section"), lax.axis_size("tensor")
    pairs = []
    for s in range(sections):
        for t in range(peers):
            chip = (t // 2 + (1 - 2 * (t % 2)) * shift) % (peers // 2)
            pairs.append((s * peers + t, ((s + by) % sections) * peers + 2 * chip + t % 2))
    return lax.ppermute(value, ("section", "tensor"), pairs)


def call(body, outs, ins, specs, scratch=(), vmem=24):
    return pl.pallas_call(
        body,
        grid=(1,),
        in_specs=specs,
        out_specs=[VMEM] * len(outs),
        out_shape=[jax.ShapeDtypeStruct(s, d) for s, d in outs],
        scratch_shapes=list(scratch),
        compiler_params=pltpu.CompilerParams(vmem_limit_bytes=vmem * 2**20),
        cost_estimate=pl.CostEstimate(flops=1, bytes_accessed=1, transcendentals=0),
    )(*ins)


def rows_of(count, index, width=WIDE):
    return pl.BlockSpec((count, width), lambda i: (index, 0))


def chunk_of(place, by, chips):
    core = place % 2
    return (place // 2 + (1 - 2 * core) * by + 2 * chips) % chips


def chunk_of_weights(w_ref, place, by, chips):
    return w_ref[:, pl.ds(pl.multiple_of(chunk_of(place, by, chips) * WIDE, WIDE), WIDE)]


def encode(value, out_ref):
    rows = value.shape[0]
    top = jnp.maximum(jnp.max(jnp.abs(value), axis=0, keepdims=True), 1e-30)
    level = jnp.ceil(jnp.log2(top) * 256.0) + 1.0
    codes = jnp.round(value * (LEVELS * jnp.exp2(level * (-1.0 / 256.0))))
    out_ref[:rows] = codes.astype(jnp.int32).astype(CODE)
    out_ref[rows:] = jnp.broadcast_to(level, (16, value.shape[1])).astype(jnp.int32).astype(CODE)


def decode(ref):
    rows = ref.shape[0] - 16
    level = ref[rows:].astype(jnp.int32).astype(F32)[:1]
    return ref[:rows].astype(jnp.int32).astype(F32) * (jnp.exp2(level * (1.0 / 256.0)) * (1.0 / LEVELS))


def project(place, plan, contexts, weights, chips):

    order = (-3, 3, -2, 2, -1, 1, 4, 0)

    def body(place_ref, plan_ref, ctx_ref, w_ref, send_ref, keep3_ref, keep2_ref, keep1_ref, keep4_ref, own_ref, held, ctx, full, sems, ctx_sem):
        here = place_ref[0]
        core = here % 2
        mine, theirs = core, 1 - core
        fetch = pltpu.make_async_copy(ctx_ref.at[plan_ref[0]], ctx, ctx_sem)
        fetch.start()
        copies = []
        for slot, by in enumerate(order):
            at = pl.multiple_of(chunk_of(here, by, chips) * WIDE, WIDE)
            copies.append(pltpu.make_async_copy(w_ref.at[:, pl.ds(at, WIDE)], held.at[slot], sems.at[slot]))
        for copy in copies:
            copy.start()
        fetch.wait()

        def product(by):
            slot = order.index(by)
            copies[slot].wait()
            return jnp.dot(ctx[...], held[slot], preferred_element_type=F32)

        for slot, (by, keep_ref) in enumerate(((3, keep3_ref), (2, keep2_ref), (1, keep1_ref))):
            send_ref[slot * ROWS : (slot + 1) * ROWS] = product(-by)
            keep_ref[...] = product(by)
        full[...] = product(4)
        send_ref[3 * ROWS : 3 * ROWS + HALF] = full[pl.ds(pl.multiple_of(theirs * HALF, HALF), HALF)]
        keep4_ref[...] = full[pl.ds(pl.multiple_of(mine * HALF, HALF), HALF)]
        full[...] = product(0)
        for part, at in ((0, 0), (1, HALF)):
            lanes = slice(part * BLOCK, (part + 1) * BLOCK)
            rows = slice(at, at + HALF)
            send_ref[3 * ROWS + HALF :, lanes] = full[rows, pl.ds(pl.multiple_of(theirs * BLOCK, BLOCK), BLOCK)]
            own_ref[:, lanes] = full[rows, pl.ds(pl.multiple_of(mine * BLOCK, BLOCK), BLOCK)]

    heads = weights.shape[0]
    return call(
        body,
        [((4 * ROWS, WIDE), F32)] + [((ROWS, WIDE), F32)] * 3 + [((HALF, WIDE), F32)] * 2,
        (place, plan, contexts, weights),
        [SMEM, SMEM, ANY, ANY],
        [
            pltpu.VMEM((8, heads, WIDE), BF16),
            pltpu.VMEM((ROWS, heads), BF16),
            pltpu.VMEM((ROWS, WIDE), F32),
            pltpu.SemaphoreType.DMA((8,)),
            pltpu.SemaphoreType.DMA,
        ],
        vmem=46,
    )


def encode_first(place, keep3, keep4, arrived):
    def body(place_ref, keep3_ref, keep4_ref, in3_ref, in4_ref, q_ref):
        encode(keep3_ref[...] + in3_ref[...], q_ref.at[: ROWS + 16])
        encode(keep4_ref[...] + in4_ref[...], q_ref.at[ROWS + 16 :])

    return call(
        body,
        [((ROWS + HALF + 32, WIDE), CODE)],
        (place, keep3, keep4, arrived, arrived),
        [SMEM, VMEM, VMEM, rows_of(ROWS, 0), rows_of(HALF, 6)],
    )[0]


def encode_two(place, keep2, keep1, arrived, q34):
    def body(place_ref, keep2_ref, keep1_ref, in2_ref, in1_ref, q34_ref, q2_ref, q1_ref, total):
        mine = pl.multiple_of((place_ref[0] % 2) * HALF, HALF)
        total[...] = keep2_ref[...] + in2_ref[...]
        total[pl.ds(mine, HALF)] += decode(q34_ref.at[ROWS + 16 :])
        encode(total[...], q2_ref)
        encode(keep1_ref[...] + in1_ref[...] + decode(q34_ref.at[: ROWS + 16]), q1_ref)

    return call(
        body,
        [((ROWS + 16, WIDE), CODE)] * 2,
        (place, keep2, keep1, arrived, arrived, q34),
        [SMEM, VMEM, VMEM, rows_of(ROWS, 1), rows_of(ROWS, 2), VMEM],
        [pltpu.VMEM((ROWS, WIDE), F32)],
    )


def gather_home(place, plan, q1, q2, own, arrived, residual):
    def body(place_ref, plan_ref, q1_ref, q2_ref, own_ref, in_ref, res_ref, send_ref, part_ref, full, stream, sem):
        fetch = pltpu.make_async_copy(res_ref.at[plan_ref[0]], stream, sem)
        fetch.start()
        core = place_ref[0] % 2
        mine = pl.multiple_of(core * BLOCK, BLOCK)
        theirs = pl.multiple_of((1 - core) * BLOCK, BLOCK)
        full[...] = decode(q1_ref) + decode(q2_ref)
        send_ref[...] = full[:, pl.ds(theirs, BLOCK)]
        fetch.wait()
        for part, at in ((0, 0), (1, HALF)):
            lanes = slice(part * BLOCK, (part + 1) * BLOCK)
            rows = slice(at, at + HALF)
            part_ref[rows] = (
                full[rows, pl.ds(mine, BLOCK)]
                + own_ref[:, lanes]
                + in_ref[:, lanes]
                + stream[rows].astype(F32)
            )

    return call(
        body,
        [((ROWS, BLOCK), F32)] * 2,
        (place, plan, q1, q2, own, arrived, residual),
        [SMEM, SMEM, VMEM, VMEM, VMEM, rows_of(HALF, 7), ANY],
        [pltpu.VMEM((ROWS, WIDE), F32), pltpu.VMEM((ROWS, BLOCK), BF16), pltpu.SemaphoreType.DMA],
    )


def times_transposed(x, w):
    return lax.dot_general(x, w, (((1,), (1,)), ((), ())), preferred_element_type=F32)


def backproject_first(place, parts, weights, chips):
    offsets = (0, -1, -2)

    def body(place_ref, u_ref, g1_ref, g2_ref, w_ref, out_ref):
        for slot, x in enumerate((u_ref, g1_ref, g2_ref)):
            term = times_transposed(x[...], chunk_of_weights(w_ref, place_ref[0], offsets[slot], chips))
            out_ref[...] = term if slot == 0 else out_ref[...] + term

    heads = weights.shape[0]
    return call(
        body,
        [((ROWS, heads), F32)],
        (place, *parts, weights),
        [SMEM] + [VMEM] * 4,
    )[0]


def backproject_rest(place, h1, h2, h34, g3, g4, start, weights, chips):
    offsets = (1, 2, 3, -3, 4)

    def body(place_ref, h1_ref, h2_ref, h34_ref, g3_ref, g4_ref, start_ref, w_ref, out_ref, facing, total):
        core = place_ref[0] % 2
        facing[pl.ds(pl.multiple_of(core * HALF, HALF), HALF)] = g4_ref[...]
        facing[pl.ds(pl.multiple_of((1 - core) * HALF, HALF), HALF)] = h34_ref[ROWS:]
        total[...] = start_ref[...]
        for slot, x in enumerate((h1_ref, h2_ref, h34_ref.at[:ROWS], g3_ref)):
            total[...] += times_transposed(x[...], chunk_of_weights(w_ref, place_ref[0], offsets[slot], chips))
        last = times_transposed(facing[...], chunk_of_weights(w_ref, place_ref[0], offsets[4], chips))
        out_ref[...] = (total[...] + last).astype(BF16)

    heads = weights.shape[0]
    return call(
        body,
        [((ROWS, heads), BF16)],
        (place, h1, h2, h34, g3, g4, start, weights),
        [SMEM] + [VMEM] * 7,
        [
            pltpu.VMEM((ROWS, WIDE), BF16),
            pltpu.VMEM((ROWS, heads), F32),
        ],
    )[0]


def on_device(weights, contexts, residual, plan, upstream):
    w_local, contexts, residual = weights[0], contexts[0], residual[0]
    at = lax.axis_index("tensor")
    place = at.astype(jnp.int32)[None]
    chips = lax.axis_size("tensor") // 2
    first = at % 2 == 0

    mate = core_swap(upstream[0])
    pair = jnp.where(
        first, jnp.concatenate([upstream[0], mate], 1), jnp.concatenate([mate, upstream[0]], 1)
    )

    begun, pair = lax.optimization_barrier((place, pair))
    send, keep3, keep2, keep1, keep4, own = project(begun, plan, contexts, w_local, chips)
    arrived = core_swap(send)
    q34 = split_shift(encode_first(place, keep3, keep4, arrived), 2)
    q2, q1 = encode_two(place, keep2, keep1, arrived, q34)
    q2, q1 = split_shift(q2, 2), split_shift(q1, 1)

    g0 = next_section(pair, -1)
    g1 = next_section(pair, -1, 1)
    g2 = split_shift(g1, 1)
    g3 = split_shift(g2, 1)
    g4 = split_shift(jnp.where(first, g2[:HALF], g2[HALF:]), 2)
    to_mate, g0 = lax.optimization_barrier((g1, g0))
    h1, h2, h34 = core_swap(to_mate), core_swap(g2), core_swap(jnp.concatenate([g3, g4], 0))
    early = backproject_first(place, (g0, g1, g2), w_local, chips)

    after, _, _, _ = lax.optimization_barrier((place, early, h1, h2))
    send, part = gather_home(after, plan, q1, q2, own, arrived, residual)
    hidden = (part + core_swap(send)).astype(BF16)
    boundary = next_section(hidden, 1)
    gradient = backproject_rest(place, h1, h2, h34, g3, g4, early, w_local, chips)
    boundary, gradient = lax.optimization_barrier((boundary, gradient))
    return (boundary[None], gradient[None])


def solution(mesh):
    return jax.shard_map(
        on_device,
        mesh=mesh,
        in_specs=(
            P("section", "tensor", None),
            P("section", None, "dp", "tensor"),
            P("section", None, "dp", "tensor"),
            P("section"),
            P("section", "dp", "tensor"),
        ),
        out_specs=(P("section", "dp", "tensor"), P("section", "dp", "tensor")),
        check_vma=False,
    )
```

```python
import jax
import jax.numpy as jnp
from jax import lax
from jax.experimental import pallas as pl
from jax.experimental.pallas import tpu as pltpu
from jax.sharding import PartitionSpec as P

ROWS = 128
HALF = 64
BLOCK = 512
WIDE = 1024
LEVELS = 32700.0
F32, BF16, CODE = jnp.float32, jnp.bfloat16, jnp.int16

SMEM = pl.BlockSpec(memory_space=pltpu.SMEM)
VMEM = pl.BlockSpec(memory_space=pltpu.VMEM)
ANY = pl.BlockSpec(memory_space=pl.ANY)


def split_shift(value, by):
    peers = lax.axis_size("tensor")
    chips = peers // 2
    pairs = []
    for chip in range(chips):
        pairs.append((2 * chip, 2 * ((chip + by) % chips)))
        pairs.append((2 * chip + 1, 2 * ((chip - by) % chips) + 1))
    return lax.ppermute(value, "tensor", pairs)


def core_swap(value):
    peers = lax.axis_size("tensor")
    return lax.ppermute(value, "tensor", [(i, i ^ 1) for i in range(peers)])


def next_section(value, by, shift=0):
    sections, peers = lax.axis_size("section"), lax.axis_size("tensor")
    pairs = []
    for s in range(sections):
        for t in range(peers):
            chip = (t // 2 + (1 - 2 * (t % 2)) * shift) % (peers // 2)
            pairs.append((s * peers + t, ((s + by) % sections) * peers + 2 * chip + t % 2))
    return lax.ppermute(value, ("section", "tensor"), pairs)


def call(body, outs, ins, specs, scratch=(), vmem=24):
    return pl.pallas_call(
        body,
        grid=(1,),
        in_specs=specs,
        out_specs=[VMEM] * len(outs),
        out_shape=[jax.ShapeDtypeStruct(s, d) for s, d in outs],
        scratch_shapes=list(scratch),
        compiler_params=pltpu.CompilerParams(vmem_limit_bytes=vmem * 2**20),
        cost_estimate=pl.CostEstimate(flops=1, bytes_accessed=1, transcendentals=0),
    )(*ins)


def rows_of(count, index, width=WIDE):
    return pl.BlockSpec((count, width), lambda i: (index, 0))


def chunk_of(place, by, chips):
    core = place % 2
    return (place // 2 + (1 - 2 * core) * by + 2 * chips) % chips


def chunk_of_weights(w_ref, place, by, chips):
    return w_ref[:, pl.ds(pl.multiple_of(chunk_of(place, by, chips) * WIDE, WIDE), WIDE)]


def encode(value, out_ref):
    rows = value.shape[0]
    top = jnp.maximum(jnp.max(jnp.abs(value), axis=0, keepdims=True), 1e-30)
    level = jnp.ceil(jnp.log2(top) * 256.0) + 1.0
    codes = jnp.round(value * (LEVELS * jnp.exp2(level * (-1.0 / 256.0))))
    out_ref[:rows] = codes.astype(jnp.int32).astype(CODE)
    out_ref[rows:] = jnp.broadcast_to(level, (16, value.shape[1])).astype(jnp.int32).astype(CODE)


def decode(ref):
    rows = ref.shape[0] - 16
    level = ref[rows:].astype(jnp.int32).astype(F32)[:1]
    return ref[:rows].astype(jnp.int32).astype(F32) * (jnp.exp2(level * (1.0 / 256.0)) * (1.0 / LEVELS))


def project(place, plan, contexts, weights, chips):

    order = (-3, 3, -2, 2, -1, 1, 4, 0)

    def body(place_ref, plan_ref, ctx_ref, w_ref, send_ref, keep3_ref, keep2_ref, keep1_ref, keep4_ref, own_ref, held, ctx, full, sems, ctx_sem):
        here = place_ref[0]
        core = here % 2
        mine, theirs = core, 1 - core
        fetch = pltpu.make_async_copy(ctx_ref.at[plan_ref[0]], ctx, ctx_sem)
        fetch.start()
        copies = []
        for slot, by in enumerate(order):
            at = pl.multiple_of(chunk_of(here, by, chips) * WIDE, WIDE)
            copies.append(pltpu.make_async_copy(w_ref.at[:, pl.ds(at, WIDE)], held.at[slot], sems.at[slot]))
        for copy in copies:
            copy.start()
        fetch.wait()

        def product(by):
            slot = order.index(by)
            copies[slot].wait()
            return jnp.dot(ctx[...], held[slot], preferred_element_type=F32)

        for slot, (by, keep_ref) in enumerate(((3, keep3_ref), (2, keep2_ref), (1, keep1_ref))):
            send_ref[slot * ROWS : (slot + 1) * ROWS] = product(-by)
            keep_ref[...] = product(by)
        full[...] = product(4)
        send_ref[3 * ROWS : 3 * ROWS + HALF] = full[pl.ds(pl.multiple_of(theirs * HALF, HALF), HALF)]
        keep4_ref[...] = full[pl.ds(pl.multiple_of(mine * HALF, HALF), HALF)]
        full[...] = product(0)
        for part, at in ((0, 0), (1, HALF)):
            lanes = slice(part * BLOCK, (part + 1) * BLOCK)
            rows = slice(at, at + HALF)
            send_ref[3 * ROWS + HALF :, lanes] = full[rows, pl.ds(pl.multiple_of(theirs * BLOCK, BLOCK), BLOCK)]
            own_ref[:, lanes] = full[rows, pl.ds(pl.multiple_of(mine * BLOCK, BLOCK), BLOCK)]

    heads = weights.shape[0]
    return call(
        body,
        [((4 * ROWS, WIDE), F32)] + [((ROWS, WIDE), F32)] * 3 + [((HALF, WIDE), F32)] * 2,
        (place, plan, contexts, weights),
        [SMEM, SMEM, ANY, ANY],
        [
            pltpu.VMEM((8, heads, WIDE), BF16),
            pltpu.VMEM((ROWS, heads), BF16),
            pltpu.VMEM((ROWS, WIDE), F32),
            pltpu.SemaphoreType.DMA((8,)),
            pltpu.SemaphoreType.DMA,
        ],
        vmem=46,
    )


def encode_first(place, keep3, keep4, arrived):
    def body(place_ref, keep3_ref, keep4_ref, in3_ref, in4_ref, q_ref):
        encode(keep3_ref[...] + in3_ref[...], q_ref.at[: ROWS + 16])
        encode(keep4_ref[...] + in4_ref[...], q_ref.at[ROWS + 16 :])

    return call(
        body,
        [((ROWS + HALF + 32, WIDE), CODE)],
        (place, keep3, keep4, arrived, arrived),
        [SMEM, VMEM, VMEM, rows_of(ROWS, 0), rows_of(HALF, 6)],
    )[0]


def encode_two(place, keep2, keep1, arrived, q34):
    def body(place_ref, keep2_ref, keep1_ref, in2_ref, in1_ref, q34_ref, q2_ref, q1_ref, total):
        mine = pl.multiple_of((place_ref[0] % 2) * HALF, HALF)
        total[...] = keep2_ref[...] + in2_ref[...]
        total[pl.ds(mine, HALF)] += decode(q34_ref.at[ROWS + 16 :])
        encode(total[...], q2_ref)
        encode(keep1_ref[...] + in1_ref[...] + decode(q34_ref.at[: ROWS + 16]), q1_ref)

    return call(
        body,
        [((ROWS + 16, WIDE), CODE)] * 2,
        (place, keep2, keep1, arrived, arrived, q34),
        [SMEM, VMEM, VMEM, rows_of(ROWS, 1), rows_of(ROWS, 2), VMEM],
        [pltpu.VMEM((ROWS, WIDE), F32)],
    )


def gather_home(place, plan, q1, q2, own, arrived, residual):
    def body(place_ref, plan_ref, q1_ref, q2_ref, own_ref, in_ref, res_ref, send_ref, part_ref, full, stream, sem):
        fetch = pltpu.make_async_copy(res_ref.at[plan_ref[0]], stream, sem)
        fetch.start()
        core = place_ref[0] % 2
        mine = pl.multiple_of(core * BLOCK, BLOCK)
        theirs = pl.multiple_of((1 - core) * BLOCK, BLOCK)
        full[...] = decode(q1_ref) + decode(q2_ref)
        send_ref[...] = full[:, pl.ds(theirs, BLOCK)]
        fetch.wait()
        for part, at in ((0, 0), (1, HALF)):
            lanes = slice(part * BLOCK, (part + 1) * BLOCK)
            rows = slice(at, at + HALF)
            part_ref[rows] = (
                full[rows, pl.ds(mine, BLOCK)]
                + own_ref[:, lanes]
                + in_ref[:, lanes]
                + stream[rows].astype(F32)
            )

    return call(
        body,
        [((ROWS, BLOCK), F32)] * 2,
        (place, plan, q1, q2, own, arrived, residual),
        [SMEM, SMEM, VMEM, VMEM, VMEM, rows_of(HALF, 7), ANY],
        [pltpu.VMEM((ROWS, WIDE), F32), pltpu.VMEM((ROWS, BLOCK), BF16), pltpu.SemaphoreType.DMA],
    )


def times_transposed(x, w):
    return lax.dot_general(x, w, (((1,), (1,)), ((), ())), preferred_element_type=F32)


def backproject_first(place, parts, weights, chips):
    offsets = (0, -1, -2)

    def body(place_ref, u_ref, g1_ref, g2_ref, w_ref, out_ref):
        for slot, x in enumerate((u_ref, g1_ref, g2_ref)):
            term = times_transposed(x[...], chunk_of_weights(w_ref, place_ref[0], offsets[slot], chips))
            out_ref[...] = term if slot == 0 else out_ref[...] + term

    heads = weights.shape[0]
    return call(
        body,
        [((ROWS, heads), F32)],
        (place, *parts, weights),
        [SMEM] + [VMEM] * 4,
    )[0]


def backproject_rest(place, h1, h2, h34, g3, g4, start, weights, chips):
    offsets = (1, 2, 3, -3, 4)

    def body(place_ref, h1_ref, h2_ref, h34_ref, g3_ref, g4_ref, start_ref, w_ref, out_ref, facing, total):
        core = place_ref[0] % 2
        facing[pl.ds(pl.multiple_of(core * HALF, HALF), HALF)] = g4_ref[...]
        facing[pl.ds(pl.multiple_of((1 - core) * HALF, HALF), HALF)] = h34_ref[ROWS:]
        total[...] = start_ref[...]
        for slot, x in enumerate((h1_ref.at[:ROWS], h2_ref, h34_ref.at[:ROWS], g3_ref)):
            total[...] += times_transposed(x[...], chunk_of_weights(w_ref, place_ref[0], offsets[slot], chips))
        last = times_transposed(facing[...], chunk_of_weights(w_ref, place_ref[0], offsets[4], chips))
        out_ref[...] = (total[...] + last).astype(BF16)

    heads = weights.shape[0]
    return call(
        body,
        [((ROWS, heads), BF16)],
        (place, h1, h2, h34, g3, g4, start, weights),
        [SMEM] + [VMEM] * 7,
        [
            pltpu.VMEM((ROWS, WIDE), BF16),
            pltpu.VMEM((ROWS, heads), F32),
        ],
    )[0]


def on_device(weights, contexts, residual, plan, upstream):
    w_local, contexts, residual = weights[0], contexts[0], residual[0]
    at = lax.axis_index("tensor")
    place = at.astype(jnp.int32)[None]
    chips = lax.axis_size("tensor") // 2
    first = at % 2 == 0

    mate = core_swap(upstream[0])
    pair = jnp.where(
        first, jnp.concatenate([upstream[0], mate], 1), jnp.concatenate([mate, upstream[0]], 1)
    )

    begun, pair = lax.optimization_barrier((place, pair))
    send, keep3, keep2, keep1, keep4, own = project(begun, plan, contexts, w_local, chips)
    arrived = core_swap(send)
    q34 = split_shift(encode_first(place, keep3, keep4, arrived), 2)
    q2, q1 = encode_two(place, keep2, keep1, arrived, q34)
    q2, q1 = split_shift(q2, 2), split_shift(q1, 1)

    g0 = next_section(pair, -1)
    g1 = next_section(pair, -1, 1)
    g2 = split_shift(g1, 1)
    g3 = split_shift(g2, 1)
    g4 = split_shift(jnp.where(first, g2[:HALF], g2[HALF:]), 2)
    h1 = core_swap(jnp.concatenate([g1, g1[: HALF // 2]], 0))
    to_mate, g0 = lax.optimization_barrier((g2, g0))
    h2, h34 = core_swap(to_mate), core_swap(jnp.concatenate([g3, g4], 0))
    early = backproject_first(place, (g0, g1, g2), w_local, chips)

    after, _, _, _ = lax.optimization_barrier((place, early, h1, h2))
    send, part = gather_home(after, plan, q1, q2, own, arrived, residual)
    hidden = (part + core_swap(send)).astype(BF16)
    boundary = next_section(hidden, 1)
    gradient = backproject_rest(place, h1, h2, h34, g3, g4, early, w_local, chips)
    boundary, gradient = lax.optimization_barrier((boundary, gradient))
    return (boundary[None], gradient[None])


def solution(mesh):
    return jax.shard_map(
        on_device,
        mesh=mesh,
        in_specs=(
            P("section", "tensor", None),
            P("section", None, "dp", "tensor"),
            P("section", None, "dp", "tensor"),
            P("section"),
            P("section", "dp", "tensor"),
        ),
        out_specs=(P("section", "dp", "tensor"), P("section", "dp", "tensor")),
        check_vma=False,
    )
```
